32 devices in a mesh: gz: 8 (over z, y), gy: 4 (over x, core).
Axes of the slice: x: 2, y: 2, z: 4, core: 2. Of those that a mesh axis runs over, the one named last changes fastest.
Arguments:
- state: bfloat16 [5, 8, 768, 1536], P(None, None, 'gy', 'gz'), may hold values from -6 to 6
- visc_base: bfloat16 [8, 768, 1536], P(None, 'gy', 'gz'), may hold values from 0.29882812 to 3
- dz_op: bfloat16 [1536, 1536], replicated, may hold values from -0.15625 to 0.15625
- dy_op: bfloat16 [768, 768], replicated, may hold values from -0.21875 to 0.21875
Outputs:
- new_state: bfloat16 [5, 8, 768, 1536], P(None, None, 'gy', 'gz')
The draws below stay inside these ranges and needn't reach their ends.
All inputs are finite; a program needn't handle non-finite values.
Results may differ from the reference program's by a relative error of at most 0.011.
Values may be sent and summed in bfloat16 or wider, within the bound.
A program may use at most 128 MiB of HBM per device.

```python
import math
import jax
import jax.numpy as jnp
from jax import lax

FIELDS = 5
X = 8
NY = 768
NZ = 1536


def levels(own_key, shape, cuts, smallest, high):
    gain, own = 1.0, jax.random.fold_in(own_key, 6)
    for dim, shards_of in cuts:
        heights = jnp.exp(jax.random.uniform(jax.random.fold_in(own, dim), (shards_of,), jnp.float32, smallest / len(cuts), high / len(cuts)))
        gain = gain * jnp.repeat(heights, shape[dim] // shards_of).reshape([-1 if axis == dim else 1 for axis in range(len(shape))])
    return gain


def bell_draw(own_key, dims, deviation, reach, pieces=(), held_as=jnp.bfloat16):
    values = jax.random.normal(own_key, dims, jnp.float32) * deviation
    if len(pieces) > 0:
        values = levels(own_key, dims, pieces, -0.22, 0.18) * values
    return jnp.clip(values, min=-reach, max=reach).astype(held_as)


def setup_inputs(seed: int = 0) -> dict:
    streams_of = jax.random.split(jax.random.key(seed), 5)
    return {
        "state": bell_draw(streams_of[0], (FIELDS, X, NY, NZ), 1.0, 6.0, ((2, 4), (3, 8))),
        "visc_base": jnp.clip(jnp.exp(math.log(3.0) - 2.306499 * jax.random.uniform(streams_of[1], (X, NY, NZ), jnp.float32) ** levels(streams_of[1], (X, NY, NZ), ((1, 4), (2, 8)), -0.2, 0.2)), 0.29882812, 3.0).astype(jnp.bfloat16),
        "dz_op": bell_draw(streams_of[2], (NZ, NZ), NZ ** -0.5, 0.15625),
        "dy_op": bell_draw(streams_of[3], (NY, NY), NY ** -0.5, 0.21875),
    }


def zline_apply(field, operator):
    result = jnp.dot(field.reshape(-1, operator.shape[0]), operator, preferred_element_type=jnp.float32)
    return result.astype(jnp.bfloat16).reshape(field.shape)


def yline_apply(field, operator):
    turned = jnp.swapaxes(field, 1, 2)
    result = jnp.dot(turned.reshape(-1, operator.shape[0]), operator, preferred_element_type=jnp.float32)
    return jnp.swapaxes(result.astype(jnp.bfloat16).reshape(turned.shape), 1, 2)


def reference(state, visc_base, dz_op, dy_op):
    grad_z = lax.map(lambda field: zline_apply(field, dz_op), state)
    grad_y = lax.map(lambda field: yline_apply(field, dy_op), state)
    sensor = grad_y[0].astype(jnp.float32) ** 2 + grad_z[0].astype(jnp.float32) ** 2
    visc = (visc_base.astype(jnp.float32) * (0.5 + sensor / (1.0 + sensor))).astype(jnp.bfloat16)
    weight = visc.astype(jnp.float32)[None]
    flux_z = (weight * grad_z.astype(jnp.float32)).astype(jnp.bfloat16)
    flux_y = (weight * grad_y.astype(jnp.float32)).astype(jnp.bfloat16)
    div_z = lax.map(lambda field: zline_apply(field, dz_op), flux_z)
    div_y = lax.map(lambda field: yline_apply(field, dy_op), flux_y)
    total = state.astype(jnp.float32) + 0.5 * (div_y.astype(jnp.float32) + div_z.astype(jnp.float32))
    return total.astype(jnp.bfloat16)
```

```python
import functools

import jax
import jax.numpy as jnp
from jax import lax
from jax.experimental import pallas as pl
from jax.experimental.pallas import tpu as pltpu
from jax.sharding import PartitionSpec as P

F32 = jnp.float32
BF16 = jnp.bfloat16
MESH = pl.DeviceIdType.MESH
LANES = 128


def apply_line(items, operator):
    shape_in = items.shape
    result = jnp.dot(
        items.reshape(-1, operator.shape[0]), operator, preferred_element_type=F32
    )
    return result.astype(BF16).reshape(shape_in)


def into_zlines(values):
    layers, planes, ylocal, zlocal = values.shape
    flattened = values.reshape(layers, planes * ylocal, zlocal)
    return lax.all_to_all(flattened, "gz", split_axis=1, concat_axis=2, tiled=True)


def from_zlines(values, planes, ylocal):
    returned = lax.all_to_all(values, "gz", split_axis=2, concat_axis=1, tiled=True)
    return returned.reshape(returned.shape[0], planes, ylocal, returned.shape[2])


def into_ylines(values):
    layers, planes, ylocal, zlocal = values.shape
    turned = jnp.swapaxes(values, 2, 3).reshape(layers, planes * zlocal, ylocal)
    return lax.all_to_all(turned, "gy", split_axis=1, concat_axis=2, tiled=True)


def from_ylines(values, planes, zlocal):
    returned = lax.all_to_all(values, "gy", split_axis=2, concat_axis=1, tiled=True)
    layers = returned.shape[0]
    return jnp.swapaxes(returned.reshape(layers, planes, zlocal, returned.shape[2]), 2, 3)


def viscosity(dens_y, dens_z, visc_base):
    sensor = dens_y.astype(F32) ** 2 + dens_z.astype(F32) ** 2
    return (visc_base.astype(F32) * (0.5 + sensor / (1.0 + sensor))).astype(BF16)


def product(visc, gradient):
    return (visc.astype(F32) * gradient.astype(F32)).astype(BF16)


def by_lines(state, visc_base, dz_op, dy_op):
    planes, ylocal, zlocal = visc_base.shape
    zline_grad = apply_line(into_zlines(state), dz_op)
    yline_grad = apply_line(into_ylines(state), dy_op)
    dens_z = from_zlines(zline_grad[0:1], planes, ylocal)
    dens_y = from_ylines(yline_grad[0:1], planes, zlocal)
    visc = viscosity(dens_y[0], dens_z[0], visc_base)
    visc_z = into_zlines(visc[None])
    visc_y = into_ylines(visc[None])
    div_z = from_zlines(apply_line(product(visc_z, zline_grad), dz_op), planes, ylocal)
    div_y = from_ylines(apply_line(product(visc_y, yline_grad), dy_op), planes, zlocal)
    total = state.astype(F32) + 0.5 * (div_y.astype(F32) + div_z.astype(F32))
    return total.astype(BF16)


def pack(block, odd):
    rows, width = block.shape[-2:]
    half, whole = rows // 2, width - LANES // 2
    cat = jnp.concatenate
    e_rest = block[..., whole:]
    even = cat([block[..., :whole], cat([e_rest[..., :half, :], e_rest[..., half:, :]], -1)], -2)
    o_rest = block[..., : LANES // 2]
    odd_ = cat(
        [block[..., LANES // 2 :], cat([o_rest[..., half:, :], o_rest[..., :half, :]], -1)], -2
    )
    return jnp.where(odd, odd_, even)


def unpack(packed, rows, odd):
    cat = jnp.concatenate
    mid = LANES // 2
    body, rest = packed[..., :rows, :], packed[..., rows:, :]
    left, right = rest[..., :mid], rest[..., mid:]
    even = cat([body, cat([left, right], -2)], -1)
    odd_ = cat([cat([right, left], -2), body], -1)
    return jnp.where(odd, odd_, even)


def kernel(
    nz, ny, fields,
    sp, dz_h, dyt_h, out,
    rin, zst, yst, gz, gy, dz, dyt, g0, visc, vy, fz, fy, dvs, dvr, osend,
    in_s, in_r, fw_s, fw_r, dv_s, dv_r, g_s, g_r, v_s, v_r, out_s, out_r, w_sem,
):
    me_z, me_y = lax.axis_index("gz"), lax.axis_index("gy")
    yl, zfull = zst.shape[1], zst.shape[2]
    zw = yst.shape[2]
    pairs = nz // 2
    pw = zfull // pairs
    half = yl // 2
    slots = fields + 1

    def loop(lo, hi, body):
        def step(k, carry):
            body(k)
            return carry

        lax.fori_loop(lo, hi, step, 0)

    def remote(src, dst, ssem, rsem, axis, peer):
        return pltpu.make_async_remote_copy(
            src_ref=src, dst_ref=dst, send_sem=ssem, recv_sem=rsem,
            device_id={axis: peer}, device_id_type=MESH,
        )

    barrier = pltpu.get_barrier_semaphore()

    def greet(axis, me, n):
        def body(d):
            pl.semaphore_signal(
                barrier, inc=1, device_id={axis: lax.rem(me + d, n)}, device_id_type=MESH
            )

        loop(1, n, body)

    w1 = pltpu.make_async_copy(dz_h, dz, w_sem.at[0])
    w2 = pltpu.make_async_copy(dyt_h, dyt, w_sem.at[1])
    greet("gz", me_z, nz)
    greet("gy", me_y, ny)
    pl.semaphore_wait(barrier, nz + ny - 2)

    def own_in(s):
        return pltpu.make_async_copy(sp.at[s, me_z], rin.at[s, me_z], in_r.at[s, me_z])

    def in_copy(s, other, slot):
        return remote(
            sp.at[s, other], rin.at[s, slot], in_s.at[s, other], in_r.at[s, slot], "gz", other
        )

    def start_in(s):
        loop(1, nz, lambda d: in_copy(s, lax.rem(me_z + d, nz), me_z).start())
        own_in(s).start()

    def wait_in(s):
        loop(1, nz, lambda d: in_copy(s, lax.rem(me_z + d, nz), lax.rem(me_z + d, nz)).wait_recv())
        own_in(s).wait()

    def zcols(j):
        return pl.ds(pl.multiple_of(j * zw, LANES), zw)

    def yrows(j):
        return pl.ds(pl.multiple_of(j * yl, 16), yl)

    class Swap:
        def __init__(self, src, dst, ssem, rsem, to_y):
            self.src, self.dst, self.ssem, self.rsem, self.to_y = src, dst, ssem, rsem, to_y

        def piece(self, j):
            return self.src.at[:, zcols(j)] if self.to_y else self.src.at[yrows(j), :]

        def place(self, j):
            return self.dst.at[yrows(j), :] if self.to_y else self.dst.at[:, zcols(j)]

        def local(self):
            return pltpu.make_async_copy(self.piece(me_y), self.place(me_y), self.rsem.at[me_y])

        def copy(self, other, slot):
            return remote(
                self.piece(other), self.place(slot), self.ssem.at[other], self.rsem.at[slot],
                "gy", other,
            )

        def start(self):
            loop(1, ny, lambda d: self.copy(lax.rem(me_y + d, ny), me_y).start())
            self.local().start()

        def wait(self):
            def body(d):
                other = lax.rem(me_y + d, ny)
                self.copy(other, other).wait_recv()

            loop(1, ny, body)
            self.local().wait()

        def sent(self):
            loop(1, ny, lambda d: self.copy(lax.rem(me_y + d, ny), me_y).wait_send())

    def forward(f, s):
        return Swap(zst.at[s], yst.at[f], fw_s.at[f], fw_r.at[f], True)

    def divs(f):
        return Swap(dvs.at[f], dvr.at[f], dv_s.at[f], dv_r.at[f], False)

    dens_y = Swap(gy.at[0], g0, g_s, g_r, False)
    visc_y = Swap(visc, vy, v_s, v_r, True)

    def out_copy(f, other, slot):
        return remote(
            osend.at[f, other], out.at[f, slot], out_s.at[f, other], out_r.at[f, slot],
            "gz", other,
        )

    def own_out(f):
        return pltpu.make_async_copy(osend.at[f, me_z], out.at[f, me_z], out_r.at[f, me_z])

    def pair_cols(m):
        return pl.multiple_of(m * pw, LANES)

    low = lax.broadcasted_iota(jnp.int32, (half, LANES), 1) < LANES // 2

    def turn(x):
        return pltpu.roll(x, LANES // 2, 1)

    def gather_lines(s):
        wait_in(s)

        def body(m):
            c = pair_cols(m)
            zst[s, :, pl.ds(c, pw // 3)] = rin[s, 2 * m, :yl, :]
            zst[s, :, pl.ds(pl.multiple_of(c + 2 * LANES, LANES), LANES)] = rin[
                s, 2 * m + 1, :yl, :
            ]
            pe = rin[s, 2 * m, yl:, :].astype(F32)
            po = rin[s, 2 * m + 1, yl:, :].astype(F32)
            mid = pl.ds(pl.multiple_of(c + LANES, LANES), LANES)
            zst[s, :half, mid] = jnp.where(low, pe, po).astype(BF16)
            zst[s, half:, mid] = turn(jnp.where(low, po, pe)).astype(BF16)

        loop(0, pairs, body)

    def grad_z(f, s):
        def body(m):
            cols = pl.ds(pair_cols(m), pw)
            gz[f, :, cols] = jnp.dot(
                zst[s], dz[:, cols], preferred_element_type=F32
            ).astype(BF16)

        loop(0, pairs, body)

    def grad_y(f):
        def body(r):
            rows = yrows(r)
            gy[f, rows, :] = jnp.dot(
                dyt[rows, :], yst[f], preferred_element_type=F32
            ).astype(BF16)

        loop(0, ny, body)

    def stage_a(f, s):
        gather_lines(s)
        forward(f, s).start()
        grad_z(f, s)

    def stage_b(f, s):
        forward(f, s).wait()
        grad_y(f)

    def viscosity_lines():
        def body(m):
            cols = pl.ds(pair_cols(m), pw)
            a, b = g0[:, cols].astype(F32), gz[0, :, cols].astype(F32)
            sensor = a * a + b * b
            visc[:, cols] = (
                zst[1, :, cols].astype(F32) * (0.5 + sensor / (1.0 + sensor))
            ).astype(BF16)

        loop(0, pairs, body)

    def stage_c(f):
        def weigh(r):
            rows = yrows(r)
            fy[rows, :] = (vy[rows, :].astype(F32) * gy[f, rows, :].astype(F32)).astype(BF16)

        loop(0, ny, weigh)

        def body(r):
            rows = yrows(r)
            dvs[f, rows, :] = jnp.dot(
                dyt[rows, :], fy[...], preferred_element_type=F32
            ).astype(BF16)

        loop(0, ny, body)
        divs(f).start()

    def stage_d(f, s):
        def weigh(m):
            cols = pl.ds(pair_cols(m), pw)
            fz[:, cols] = (visc[:, cols].astype(F32) * gz[f, :, cols].astype(F32)).astype(BF16)

        loop(0, pairs, weigh)
        divs(f).wait()

        def body(m):
            cols = pl.ds(pair_cols(m), pw)
            div = jnp.dot(fz[...], dz[:, cols], preferred_element_type=F32)
            div = div.astype(BF16).astype(F32)
            new = zst[s, :, cols].astype(F32) + 0.5 * (dvr[f, :, cols].astype(F32) + div)
            osend[f, 2 * m, :yl, :] = new[:, :LANES].astype(BF16)
            osend[f, 2 * m + 1, :yl, :] = new[:, 2 * LANES :].astype(BF16)
            top = new[:half, LANES : 2 * LANES]
            bottom = turn(new[half:, LANES : 2 * LANES])
            osend[f, 2 * m, yl:, :] = jnp.where(low, top, bottom).astype(BF16)
            osend[f, 2 * m + 1, yl:, :] = jnp.where(low, bottom, top).astype(BF16)

        loop(0, pairs, body)
        loop(1, nz, lambda d: out_copy(f, lax.rem(me_z + d, nz), me_z).start())
        own_out(f).start()

    loop(0, slots, start_in)
    w1.start()
    w2.start()
    w1.wait()
    w2.wait()
    stage_a(0, 0)
    stage_b(0, 0)
    dens_y.start()
    gather_lines(1)
    dens_y.wait()
    viscosity_lines()
    visc_y.start()
    stage_a(1, 2)
    stage_b(1, 2)
    visc_y.wait()

    def field(f):
        stage_c(f)

        @pl.when(f + 2 < fields)
        def _():
            stage_a(f + 2, f + 3)

        stage_d(f, jnp.where(f == 0, 0, f + 1))

        @pl.when(f + 2 < fields)
        def _():
            stage_b(f + 2, f + 3)

    loop(0, fields, field)

    def sent_in(s):
        loop(1, nz, lambda d: in_copy(s, lax.rem(me_z + d, nz), me_z).wait_send())

    loop(0, slots, sent_in)
    dens_y.sent()
    visc_y.sent()

    def finish(f):
        forward(f, jnp.where(f == 0, 0, f + 1)).sent()
        divs(f).sent()

        def body(d):
            other = lax.rem(me_z + d, nz)
            out_copy(f, other, other).wait_recv()
            out_copy(f, other, me_z).wait_send()

        loop(1, nz, body)
        own_out(f).wait()

    loop(0, fields, finish)


def by_planes(nz, ny, state, visc_base, dz_op, dy_op):
    fields, planes, yl, zl = state.shape
    zfull, yfull = dz_op.shape[0], dy_op.shape[0]
    zw = zfull // ny
    slots = fields + 1
    prow = yl + yl // 2
    odd = lax.rem(lax.axis_index("gz"), 2) == 1
    sp = pack(jnp.concatenate([state[:1], visc_base[None], state[1:]], 0), odd)
    any_ = pl.BlockSpec(memory_space=pl.ANY)
    vm = lambda *shape: pltpu.VMEM(shape, BF16)
    dma = lambda *shape: pltpu.SemaphoreType.DMA(shape)
    packed = pl.pallas_call(
        functools.partial(kernel, nz, ny, fields),
        out_shape=jax.ShapeDtypeStruct((fields, planes, prow, LANES), BF16),
        in_specs=[any_] * 3,
        out_specs=any_,
        scratch_shapes=[
            vm(slots, nz, prow, LANES),
            vm(slots, yl, zfull),
            vm(fields, yfull, zw),
            vm(fields, yl, zfull),
            vm(fields, yfull, zw),
            vm(zfull, zfull),
            vm(yfull, yfull),
            vm(yl, zfull),
            vm(yl, zfull),
            vm(yfull, zw),
            vm(yl, zfull),
            vm(yfull, zw),
            vm(fields, yfull, zw),
            vm(fields, yl, zfull),
            vm(fields, nz, prow, LANES),
            dma(slots, nz), dma(slots, nz),
            dma(fields, ny), dma(fields, ny),
            dma(fields, ny), dma(fields, ny),
            dma(ny), dma(ny), dma(ny), dma(ny),
            dma(fields, nz), dma(fields, nz),
            dma(2),
        ],
        compiler_params=pltpu.CompilerParams(
            collective_id=0, has_side_effects=True, vmem_limit_bytes=56 * 2**20
        ),
    )(sp, dz_op, dy_op.T)
    return unpack(packed, yl, odd)


def on_device(nz, ny, state, visc_base, dz_op, dy_op):
    planes, yl, zl = visc_base.shape
    if planes == nz and nz % 2 == 0 and zl == LANES + LANES // 2 and yl % 32 == 0:
        if dz_op.shape[0] % (LANES * ny) == 0:
            return by_planes(nz, ny, state, visc_base, dz_op, dy_op)
    return by_lines(state, visc_base, dz_op, dy_op)


def solution(mesh):
    return jax.shard_map(
        functools.partial(on_device, mesh.shape["gz"], mesh.shape["gy"]),
        mesh=mesh,
        in_specs=(P(None, None, "gy", "gz"), P(None, "gy", "gz"), P(), P()),
        out_specs=P(None, None, "gy", "gz"),
        check_vma=False,
    )
```

```python
import functools

import jax
import jax.numpy as jnp
from jax import lax
from jax.experimental import pallas as pl
from jax.experimental.pallas import tpu as pltpu
from jax.sharding import PartitionSpec as P

F32 = jnp.float32
BF16 = jnp.bfloat16
MESH = pl.DeviceIdType.MESH
LANES = 128


def apply_line(items, operator):
    shape_in = items.shape
    result = jnp.dot(
        items.reshape(-1, operator.shape[0]), operator, preferred_element_type=F32
    )
    return result.astype(BF16).reshape(shape_in)


def into_zlines(values):
    layers, planes, ylocal, zlocal = values.shape
    flattened = values.reshape(layers, planes * ylocal, zlocal)
    return lax.all_to_all(flattened, "gz", split_axis=1, concat_axis=2, tiled=True)


def from_zlines(values, planes, ylocal):
    returned = lax.all_to_all(values, "gz", split_axis=2, concat_axis=1, tiled=True)
    return returned.reshape(returned.shape[0], planes, ylocal, returned.shape[2])


def into_ylines(values):
    layers, planes, ylocal, zlocal = values.shape
    turned = jnp.swapaxes(values, 2, 3).reshape(layers, planes * zlocal, ylocal)
    return lax.all_to_all(turned, "gy", split_axis=1, concat_axis=2, tiled=True)


def from_ylines(values, planes, zlocal):
    returned = lax.all_to_all(values, "gy", split_axis=2, concat_axis=1, tiled=True)
    layers = returned.shape[0]
    return jnp.swapaxes(returned.reshape(layers, planes, zlocal, returned.shape[2]), 2, 3)


def viscosity(dens_y, dens_z, visc_base):
    sensor = dens_y.astype(F32) ** 2 + dens_z.astype(F32) ** 2
    return (visc_base.astype(F32) * (0.5 + sensor / (1.0 + sensor))).astype(BF16)


def product(visc, gradient):
    return (visc.astype(F32) * gradient.astype(F32)).astype(BF16)


def by_lines(state, visc_base, dz_op, dy_op):
    planes, ylocal, zlocal = visc_base.shape
    zline_grad = apply_line(into_zlines(state), dz_op)
    yline_grad = apply_line(into_ylines(state), dy_op)
    dens_z = from_zlines(zline_grad[0:1], planes, ylocal)
    dens_y = from_ylines(yline_grad[0:1], planes, zlocal)
    visc = viscosity(dens_y[0], dens_z[0], visc_base)
    visc_z = into_zlines(visc[None])
    visc_y = into_ylines(visc[None])
    div_z = from_zlines(apply_line(product(visc_z, zline_grad), dz_op), planes, ylocal)
    div_y = from_ylines(apply_line(product(visc_y, yline_grad), dy_op), planes, zlocal)
    total = state.astype(F32) + 0.5 * (div_y.astype(F32) + div_z.astype(F32))
    return total.astype(BF16)


def kernel(
    nz, ny, fields,
    st_h, vb_h, dz_h, dy_h, out,
    cells, sp, rout, result, dyv, rin, zst, yst, gz, gy, dz, dyt, g0, visc, vy, fz, fy, dvs, dvr, osend,
    in_s, in_r, fw_s, fw_r, dv_s, dv_r, g_s, g_r, v_s, v_r, out_s, out_r, w_sem, c_sem, o_sem,
):
    me_z, me_y = lax.axis_index("gz"), lax.axis_index("gy")
    yl, zfull = zst.shape[1], zst.shape[2]
    zw = yst.shape[2]
    pairs = nz // 2
    pw = zfull // pairs
    half = yl // 2
    slots = fields + 1
    odd = lax.rem(me_z, 2)
    low = lax.broadcasted_iota(jnp.int32, (half, LANES), 1) < LANES // 2
    low_all = lax.broadcasted_iota(jnp.int32, (yl, LANES), 1) < LANES // 2

    def turn(x):
        return pltpu.roll(x, LANES // 2, 1)

    def loop(lo, hi, body):
        def step(k, carry):
            body(k)
            return carry

        lax.fori_loop(lo, hi, step, 0)

    def remote(src, dst, ssem, rsem, axis, peer):
        return pltpu.make_async_remote_copy(
            src_ref=src, dst_ref=dst, send_sem=ssem, recv_sem=rsem,
            device_id={axis: peer}, device_id_type=MESH,
        )

    barrier = pltpu.get_barrier_semaphore()

    def greet(axis, me, n):
        def body(d):
            pl.semaphore_signal(
                barrier, inc=1, device_id={axis: lax.rem(me + d, n)}, device_id_type=MESH
            )

        loop(1, n, body)

    w1 = pltpu.make_async_copy(dz_h, dz, w_sem.at[0])
    w2 = pltpu.make_async_copy(dy_h, dyv, w_sem.at[1])
    def fetch(s):
        if s == 1:
            return pltpu.make_async_copy(vb_h, cells.at[s], c_sem.at[s])
        return pltpu.make_async_copy(st_h.at[max(s - 1, 0)], cells.at[s], c_sem.at[s])

    for s in range(slots):
        fetch(s).start()
    w2.start()
    w1.start()
    greet("gz", me_z, nz)
    greet("gy", me_y, ny)
    pl.semaphore_wait(barrier, nz + ny - 2)

    def own_in(s):
        return pltpu.make_async_copy(sp.at[s, me_z], rin.at[s, me_z], in_r.at[s, me_z])

    def in_copy(s, other, slot):
        return remote(
            sp.at[s, other], rin.at[s, slot], in_s.at[s, other], in_r.at[s, slot], "gz", other
        )

    def fold(s, x):
        t0 = cells[s, x, :, :LANES].astype(F32)
        rest = cells[s, x, :, LANES:].astype(F32)
        tt = jnp.concatenate([rest, rest], axis=1)

        @pl.when(odd == 0)
        def _():
            sp[s, x, :yl, :] = t0.astype(BF16)
            sp[s, x, yl:, :] = jnp.where(low, tt[:half], tt[half:]).astype(BF16)

        @pl.when(odd == 1)
        def _():
            r0 = turn(t0)
            sp[s, x, :yl, :] = jnp.where(low_all, r0, tt).astype(BF16)
            sp[s, x, yl:, :] = jnp.where(low, t0[half:], r0[:half]).astype(BF16)

    def start_in(s):
        fetch(s).wait()

        def body(d):
            other = lax.rem(me_z + d, nz)
            fold(s, other)
            in_copy(s, other, me_z).start()

        loop(1, nz, body)
        fold(s, me_z)
        own_in(s).start()

    def unfold(f, x):
        body, rest = rout[f, x, :yl, :].astype(F32), rout[f, x, yl:, :].astype(F32)
        mid = LANES // 2

        @pl.when(odd == 0)
        def _():
            result[f, x, :, :LANES] = body.astype(BF16)
            result[f, x, :half, LANES:] = rest[:, :mid].astype(BF16)
            result[f, x, half:, LANES:] = turn(rest)[:, :mid].astype(BF16)

        @pl.when(odd == 1)
        def _():
            rb = turn(body)
            result[f, x, :half, :LANES] = jnp.where(low, turn(rest), rb[:half]).astype(BF16)
            result[f, x, half:, :LANES] = jnp.where(low, rest, rb[half:]).astype(BF16)
            result[f, x, :, LANES:] = rb[:, :mid].astype(BF16)

    def transpose_dy():
        def body(k):
            c = pl.multiple_of(k * LANES, LANES)
            dyt[pl.ds(c, LANES), :] = jnp.transpose(dyv[:, pl.ds(c, LANES)])

        loop(0, dyv.shape[0] // LANES, body)

    def wait_in(s):
        loop(1, nz, lambda d: in_copy(s, lax.rem(me_z + d, nz), lax.rem(me_z + d, nz)).wait_recv())
        own_in(s).wait()

    def zcols(j):
        return pl.ds(pl.multiple_of(j * zw, LANES), zw)

    def yrows(j):
        return pl.ds(pl.multiple_of(j * yl, 16), yl)

    class Swap:
        def __init__(self, src, dst, ssem, rsem, to_y):
            self.src, self.dst, self.ssem, self.rsem, self.to_y = src, dst, ssem, rsem, to_y

        def piece(self, j):
            return self.src.at[:, zcols(j)] if self.to_y else self.src.at[yrows(j), :]

        def place(self, j):
            return self.dst.at[yrows(j), :] if self.to_y else self.dst.at[:, zcols(j)]

        def local(self):
            return pltpu.make_async_copy(self.piece(me_y), self.place(me_y), self.rsem.at[me_y])

        def copy(self, other, slot):
            return remote(
                self.piece(other), self.place(slot), self.ssem.at[other], self.rsem.at[slot],
                "gy", other,
            )

        def start(self):
            loop(1, ny, lambda d: self.copy(lax.rem(me_y + d, ny), me_y).start())
            self.local().start()

        def wait(self):
            def body(d):
                other = lax.rem(me_y + d, ny)
                self.copy(other, other).wait_recv()

            loop(1, ny, body)
            self.local().wait()

        def sent(self):
            loop(1, ny, lambda d: self.copy(lax.rem(me_y + d, ny), me_y).wait_send())

    def forward(f, s):
        return Swap(zst.at[s], yst.at[f], fw_s.at[f], fw_r.at[f], True)

    def divs(f):
        return Swap(dvs.at[f], dvr.at[f], dv_s.at[f], dv_r.at[f], False)

    dens_y = Swap(gy.at[0], g0, g_s, g_r, False)
    visc_y = Swap(visc, vy, v_s, v_r, True)

    def out_copy(f, other, slot):
        return remote(
            osend.at[f, other], rout.at[f, slot], out_s.at[f, other], out_r.at[f, slot],
            "gz", other,
        )

    def own_out(f):
        return pltpu.make_async_copy(osend.at[f, me_z], rout.at[f, me_z], out_r.at[f, me_z])

    def pair_cols(m):
        return pl.multiple_of(m * pw, LANES)

    def gather_lines(s):
        wait_in(s)

        def body(m):
            c = pair_cols(m)
            zst[s, :, pl.ds(c, pw // 3)] = rin[s, 2 * m, :yl, :]
            zst[s, :, pl.ds(pl.multiple_of(c + 2 * LANES, LANES), LANES)] = rin[
                s, 2 * m + 1, :yl, :
            ]
            pe = rin[s, 2 * m, yl:, :].astype(F32)
            po = rin[s, 2 * m + 1, yl:, :].astype(F32)
            mid = pl.ds(pl.multiple_of(c + LANES, LANES), LANES)
            zst[s, :half, mid] = jnp.where(low, pe, po).astype(BF16)
            zst[s, half:, mid] = turn(jnp.where(low, po, pe)).astype(BF16)

        loop(0, pairs, body)

    def grad_z(f, s):
        def body(m):
            cols = pl.ds(pair_cols(m), pw)
            gz[f, :, cols] = jnp.dot(
                zst[s], dz[:, cols], preferred_element_type=F32
            ).astype(BF16)

        loop(0, pairs, body)

    def grad_y(f):
        def body(r):
            rows = yrows(r)
            gy[f, rows, :] = jnp.dot(
                dyt[rows, :], yst[f], preferred_element_type=F32
            ).astype(BF16)

        loop(0, ny, body)

    def stage_a(f, s):
        gather_lines(s)
        forward(f, s).start()
        grad_z(f, s)

    def stage_b(f, s):
        forward(f, s).wait()
        grad_y(f)

    def viscosity_lines():
        def body(m):
            cols = pl.ds(pair_cols(m), pw)
            a, b = g0[:, cols].astype(F32), gz[0, :, cols].astype(F32)
            sensor = a * a + b * b
            visc[:, cols] = (
                zst[1, :, cols].astype(F32) * (0.5 + sensor / (1.0 + sensor))
            ).astype(BF16)

        loop(0, pairs, body)

    def stage_c(f):
        def weigh(r):
            rows = yrows(r)
            fy[rows, :] = (vy[rows, :].astype(F32) * gy[f, rows, :].astype(F32)).astype(BF16)

        loop(0, ny, weigh)

        def body(r):
            rows = yrows(r)
            dvs[f, rows, :] = jnp.dot(
                dyt[rows, :], fy[...], preferred_element_type=F32
            ).astype(BF16)

        loop(0, ny, body)
        divs(f).start()

    def stage_d(f, s):
        def weigh(m):
            cols = pl.ds(pair_cols(m), pw)
            fz[:, cols] = (visc[:, cols].astype(F32) * gz[f, :, cols].astype(F32)).astype(BF16)

        loop(0, pairs, weigh)
        divs(f).wait()

        def body(m):
            cols = pl.ds(pair_cols(m), pw)
            div = jnp.dot(fz[...], dz[:, cols], preferred_element_type=F32)
            div = div.astype(BF16).astype(F32)
            new = zst[s, :, cols].astype(F32) + 0.5 * (dvr[f, :, cols].astype(F32) + div)
            osend[f, 2 * m, :yl, :] = new[:, :LANES].astype(BF16)
            osend[f, 2 * m + 1, :yl, :] = new[:, 2 * LANES :].astype(BF16)
            top = new[:half, LANES : 2 * LANES]
            bottom = turn(new[half:, LANES : 2 * LANES])
            osend[f, 2 * m, yl:, :] = jnp.where(low, top, bottom).astype(BF16)
            osend[f, 2 * m + 1, yl:, :] = jnp.where(low, bottom, top).astype(BF16)

        loop(0, pairs, body)
        loop(1, nz, lambda d: out_copy(f, lax.rem(me_z + d, nz), me_z).start())
        own_out(f).start()

    for s in range(slots):
        start_in(s)
    w2.wait()
    transpose_dy()
    w1.wait()
    stage_a(0, 0)
    stage_b(0, 0)
    dens_y.start()
    gather_lines(1)
    dens_y.wait()
    viscosity_lines()
    visc_y.start()
    stage_a(1, 2)
    stage_b(1, 2)
    visc_y.wait()

    def field(f):
        stage_c(f)

        @pl.when(f + 2 < fields)
        def _():
            stage_a(f + 2, f + 3)

        stage_d(f, jnp.where(f == 0, 0, f + 1))

        @pl.when(f + 2 < fields)
        def _():
            stage_b(f + 2, f + 3)

    loop(0, fields, field)

    def sent_in(s):
        loop(1, nz, lambda d: in_copy(s, lax.rem(me_z + d, nz), me_z).wait_send())

    loop(0, slots, sent_in)
    dens_y.sent()
    visc_y.sent()

    def finish(f):
        forward(f, jnp.where(f == 0, 0, f + 1)).sent()
        divs(f).sent()

        def body(d):
            other = lax.rem(me_z + d, nz)
            out_copy(f, other, other).wait_recv()
            unfold(f, other)
            out_copy(f, other, me_z).wait_send()

        own_out(f).wait()
        unfold(f, me_z)
        loop(1, nz, body)
        store(f).start()

    def store(f):
        return pltpu.make_async_copy(result.at[f], out.at[f], o_sem.at[f])

    loop(0, fields, finish)
    loop(0, fields, lambda f: store(f).wait())


def by_planes(nz, ny, state, visc_base, dz_op, dy_op):
    fields, planes, yl, zl = state.shape
    zfull, yfull = dz_op.shape[0], dy_op.shape[0]
    zw = zfull // ny
    slots = fields + 1
    prow = yl + yl // 2
    any_ = pl.BlockSpec(memory_space=pl.ANY)
    vm = lambda *shape: pltpu.VMEM(shape, BF16)
    dma = lambda *shape: pltpu.SemaphoreType.DMA(shape)
    return pl.pallas_call(
        functools.partial(kernel, nz, ny, fields),
        out_shape=jax.ShapeDtypeStruct(state.shape, BF16),
        in_specs=[any_] * 4,
        out_specs=any_,
        scratch_shapes=[
            vm(slots, planes, yl, zl),
            vm(slots, nz, prow, LANES),
            vm(fields, nz, prow, LANES),
            vm(fields, planes, yl, zl),
            vm(yfull, yfull),
            vm(slots, nz, prow, LANES),
            vm(slots, yl, zfull),
            vm(fields, yfull, zw),
            vm(fields, yl, zfull),
            vm(fields, yfull, zw),
            vm(zfull, zfull),
            vm(yfull, yfull),
            vm(yl, zfull),
            vm(yl, zfull),
            vm(yfull, zw),
            vm(yl, zfull),
            vm(yfull, zw),
            vm(fields, yfull, zw),
            vm(fields, yl, zfull),
            vm(fields, nz, prow, LANES),
            dma(slots, nz), dma(slots, nz),
            dma(fields, ny), dma(fields, ny),
            dma(fields, ny), dma(fields, ny),
            dma(ny), dma(ny), dma(ny), dma(ny),
            dma(fields, nz), dma(fields, nz),
            dma(2), dma(slots), dma(fields),
        ],
        compiler_params=pltpu.CompilerParams(
            collective_id=0, has_side_effects=True, vmem_limit_bytes=56 * 2**20
        ),
    )(state, visc_base, dz_op, dy_op)


def on_device(nz, ny, state, visc_base, dz_op, dy_op):
    planes, yl, zl = visc_base.shape
    if planes == nz and nz % 2 == 0 and zl == LANES + LANES // 2 and yl % 32 == 0:
        if dz_op.shape[0] % (LANES * ny) == 0:
            return by_planes(nz, ny, state, visc_base, dz_op, dy_op)
    return by_lines(state, visc_base, dz_op, dy_op)


def solution(mesh):
    return jax.shard_map(
        functools.partial(on_device, mesh.shape["gz"], mesh.shape["gy"]),
        mesh=mesh,
        in_specs=(P(None, None, "gy", "gz"), P(None, "gy", "gz"), P(), P()),
        out_specs=P(None, None, "gy", "gz"),
        check_vma=False,
    )
```

```python
import functools

import jax
import jax.numpy as jnp
from jax import lax
from jax.experimental import pallas as pl
from jax.experimental.pallas import tpu as pltpu
from jax.sharding import PartitionSpec as P

F32 = jnp.float32
BF16 = jnp.bfloat16
MESH = pl.DeviceIdType.MESH
LANES = 128


def apply_line(items, operator):
    shape_in = items.shape
    result = jnp.dot(
        items.reshape(-1, operator.shape[0]), operator, preferred_element_type=F32
    )
    return result.astype(BF16).reshape(shape_in)


def into_zlines(values):
    layers, planes, ylocal, zlocal = values.shape
    flattened = values.reshape(layers, planes * ylocal, zlocal)
    return lax.all_to_all(flattened, "gz", split_axis=1, concat_axis=2, tiled=True)


def from_zlines(values, planes, ylocal):
    returned = lax.all_to_all(values, "gz", split_axis=2, concat_axis=1, tiled=True)
    return returned.reshape(returned.shape[0], planes, ylocal, returned.shape[2])


def into_ylines(values):
    layers, planes, ylocal, zlocal = values.shape
    turned = jnp.swapaxes(values, 2, 3).reshape(layers, planes * zlocal, ylocal)
    return lax.all_to_all(turned, "gy", split_axis=1, concat_axis=2, tiled=True)


def from_ylines(values, planes, zlocal):
    returned = lax.all_to_all(values, "gy", split_axis=2, concat_axis=1, tiled=True)
    layers = returned.shape[0]
    return jnp.swapaxes(returned.reshape(layers, planes, zlocal, returned.shape[2]), 2, 3)


def viscosity(dens_y, dens_z, visc_base):
    sensor = dens_y.astype(F32) ** 2 + dens_z.astype(F32) ** 2
    return (visc_base.astype(F32) * (0.5 + sensor / (1.0 + sensor))).astype(BF16)


def product(visc, gradient):
    return (visc.astype(F32) * gradient.astype(F32)).astype(BF16)


def by_lines(state, visc_base, dz_op, dy_op):
    planes, ylocal, zlocal = visc_base.shape
    zline_grad = apply_line(into_zlines(state), dz_op)
    yline_grad = apply_line(into_ylines(state), dy_op)
    dens_z = from_zlines(zline_grad[0:1], planes, ylocal)
    dens_y = from_ylines(yline_grad[0:1], planes, zlocal)
    visc = viscosity(dens_y[0], dens_z[0], visc_base)
    visc_z = into_zlines(visc[None])
    visc_y = into_ylines(visc[None])
    div_z = from_zlines(apply_line(product(visc_z, zline_grad), dz_op), planes, ylocal)
    div_y = from_ylines(apply_line(product(visc_y, yline_grad), dy_op), planes, zlocal)
    total = state.astype(F32) + 0.5 * (div_y.astype(F32) + div_z.astype(F32))
    return total.astype(BF16)


def kernel(
    nz, ny, fields,
    st_h, vb_h, dz_h, dy_h, out,
    cells, sp, rout, dyv, rin, zst, yst, gz, gy, dz, dyt, g0, visc, vy, fz, fy, dvs, dvr, osend,
    in_s, in_r, fw_s, fw_r, dv_s, dv_r, g_s, g_r, v_s, v_r, out_s, out_r, w_sem, c_sem,
):
    me_z, me_y = lax.axis_index("gz"), lax.axis_index("gy")
    yl, zfull = zst.shape[1], zst.shape[2]
    zw = yst.shape[2]
    pairs = nz // 2
    pw = zfull // pairs
    half = yl // 2
    slots = fields + 1
    odd = lax.rem(me_z, 2)
    low = lax.broadcasted_iota(jnp.int32, (half, LANES), 1) < LANES // 2
    low_all = lax.broadcasted_iota(jnp.int32, (yl, LANES), 1) < LANES // 2

    def turn(x):
        return pltpu.roll(x, LANES // 2, 1)

    def loop(lo, hi, body):
        def step(k, carry):
            body(k)
            return carry

        lax.fori_loop(lo, hi, step, 0)

    def remote(src, dst, ssem, rsem, axis, peer):
        return pltpu.make_async_remote_copy(
            src_ref=src, dst_ref=dst, send_sem=ssem, recv_sem=rsem,
            device_id={axis: peer}, device_id_type=MESH,
        )

    barrier = pltpu.get_barrier_semaphore()

    def greet(axis, me, n):
        def body(d):
            pl.semaphore_signal(
                barrier, inc=1, device_id={axis: lax.rem(me + d, n)}, device_id_type=MESH
            )

        loop(1, n, body)

    w1 = pltpu.make_async_copy(dz_h, dz, w_sem.at[0])
    w2 = pltpu.make_async_copy(dy_h, dyv, w_sem.at[1])

    def fetch(s):
        if s == 1:
            return pltpu.make_async_copy(vb_h, cells.at[s], c_sem.at[s])
        return pltpu.make_async_copy(st_h.at[max(s - 1, 0)], cells.at[s], c_sem.at[s])

    fetch(0).start()
    greet("gz", me_z, nz)
    greet("gy", me_y, ny)
    fetch(0).wait()
    for s in range(1, slots):
        fetch(s).start()
    w2.start()
    w1.start()

    def own_in(s):
        return pltpu.make_async_copy(sp.at[s, me_z], rin.at[s, me_z], in_r.at[s, me_z])

    def in_copy(s, other, slot):
        return remote(
            sp.at[s, other], rin.at[s, slot], in_s.at[s, other], in_r.at[s, slot], "gz", other
        )

    def fold(s, x):
        t0 = cells[s, x, :, :LANES].astype(F32)
        rest = cells[s, x, :, LANES:].astype(F32)
        tt = jnp.concatenate([rest, rest], axis=1)

        @pl.when(odd == 0)
        def _():
            sp[s, x, :yl, :] = t0.astype(BF16)
            sp[s, x, yl:, :] = jnp.where(low, tt[:half], tt[half:]).astype(BF16)

        @pl.when(odd == 1)
        def _():
            r0 = turn(t0)
            sp[s, x, :yl, :] = jnp.where(low_all, r0, tt).astype(BF16)
            sp[s, x, yl:, :] = jnp.where(low, t0[half:], r0[:half]).astype(BF16)

    def start_in(s):
        if s > 0:
            fetch(s).wait()

        def body(d):
            other = lax.rem(me_z + d, nz)
            if s > 0:
                fold(s, other)
            in_copy(s, other, me_z).start()

        if s == 0:
            loop(0, nz, lambda x: fold(s, x))
            pl.semaphore_wait(barrier, nz + ny - 2)
        loop(1, nz, body)
        if s > 0:
            fold(s, me_z)
        own_in(s).start()

    def unfold(f, x):
        body, rest = rout[f, x, :yl, :].astype(F32), rout[f, x, yl:, :].astype(F32)
        mid = LANES // 2

        @pl.when(odd == 0)
        def _():
            out[f, x, :, :LANES] = body.astype(BF16)
            out[f, x, :half, LANES:] = rest[:, :mid].astype(BF16)
            out[f, x, half:, LANES:] = turn(rest)[:, :mid].astype(BF16)

        @pl.when(odd == 1)
        def _():
            rb = turn(body)
            out[f, x, :half, :LANES] = jnp.where(low, turn(rest), rb[:half]).astype(BF16)
            out[f, x, half:, :LANES] = jnp.where(low, rest, rb[half:]).astype(BF16)
            out[f, x, :, LANES:] = rb[:, :mid].astype(BF16)

    def transpose_dy():
        def body(k):
            c = pl.multiple_of(k * LANES, LANES)
            dyt[pl.ds(c, LANES), :] = jnp.transpose(dyv[:, pl.ds(c, LANES)])

        loop(0, dyv.shape[0] // LANES, body)

    def wait_in(s):
        loop(1, nz, lambda d: in_copy(s, lax.rem(me_z + d, nz), lax.rem(me_z + d, nz)).wait_recv())
        own_in(s).wait()

    def zcols(j):
        return pl.ds(pl.multiple_of(j * zw, LANES), zw)

    def yrows(j):
        return pl.ds(pl.multiple_of(j * yl, 16), yl)

    class Swap:
        def __init__(self, src, dst, ssem, rsem, to_y):
            self.src, self.dst, self.ssem, self.rsem, self.to_y = src, dst, ssem, rsem, to_y

        def piece(self, j):
            return self.src.at[:, zcols(j)] if self.to_y else self.src.at[yrows(j), :]

        def place(self, j):
            return self.dst.at[yrows(j), :] if self.to_y else self.dst.at[:, zcols(j)]

        def local(self):
            return pltpu.make_async_copy(self.piece(me_y), self.place(me_y), self.rsem.at[me_y])

        def copy(self, other, slot):
            return remote(
                self.piece(other), self.place(slot), self.ssem.at[other], self.rsem.at[slot],
                "gy", other,
            )

        def start(self):
            loop(1, ny, lambda d: self.copy(lax.rem(me_y + d, ny), me_y).start())
            self.local().start()

        def wait(self):
            def body(d):
                other = lax.rem(me_y + d, ny)
                self.copy(other, other).wait_recv()

            loop(1, ny, body)
            self.local().wait()

        def sent(self):
            loop(1, ny, lambda d: self.copy(lax.rem(me_y + d, ny), me_y).wait_send())

    def forward(f, s):
        return Swap(zst.at[s], yst.at[f], fw_s.at[f], fw_r.at[f], True)

    def divs(f):
        return Swap(dvs.at[f], dvr.at[f], dv_s.at[f], dv_r.at[f], False)

    dens_y = Swap(gy.at[0], g0, g_s, g_r, False)
    visc_y = Swap(visc, vy, v_s, v_r, True)

    def out_copy(f, other, slot):
        return remote(
            osend.at[f, other], rout.at[f, slot], out_s.at[f, other], out_r.at[f, slot],
            "gz", other,
        )

    def own_out(f):
        return pltpu.make_async_copy(osend.at[f, me_z], rout.at[f, me_z], out_r.at[f, me_z])

    def pair_cols(m):
        return pl.multiple_of(m * pw, LANES)

    def gather_lines(s):
        wait_in(s)

        def body(m):
            c = pair_cols(m)
            zst[s, :, pl.ds(c, pw // 3)] = rin[s, 2 * m, :yl, :]
            zst[s, :, pl.ds(pl.multiple_of(c + 2 * LANES, LANES), LANES)] = rin[
                s, 2 * m + 1, :yl, :
            ]
            pe = rin[s, 2 * m, yl:, :].astype(F32)
            po = rin[s, 2 * m + 1, yl:, :].astype(F32)
            mid = pl.ds(pl.multiple_of(c + LANES, LANES), LANES)
            zst[s, :half, mid] = jnp.where(low, pe, po).astype(BF16)
            zst[s, half:, mid] = turn(jnp.where(low, po, pe)).astype(BF16)

        loop(0, pairs, body)

    def grad_z(f, s):
        def body(m):
            cols = pl.ds(pair_cols(m), pw)
            gz[f, :, cols] = jnp.dot(
                zst[s], dz[:, cols], preferred_element_type=F32
            ).astype(BF16)

        loop(0, pairs, body)

    def grad_y(f):
        def body(r):
            rows = yrows(r)
            gy[f, rows, :] = jnp.dot(
                dyt[rows, :], yst[f], preferred_element_type=F32
            ).astype(BF16)

        loop(0, ny, body)

    def stage_a(f, s):
        gather_lines(s)
        forward(f, s).start()
        grad_z(f, s)

    def stage_b(f, s):
        forward(f, s).wait()
        grad_y(f)

    def viscosity_lines():
        def body(m):
            cols = pl.ds(pair_cols(m), pw)
            a, b = g0[:, cols].astype(F32), gz[0, :, cols].astype(F32)
            sensor = a * a + b * b
            visc[:, cols] = (
                zst[1, :, cols].astype(F32) * (0.5 + sensor / (1.0 + sensor))
            ).astype(BF16)

        loop(0, pairs, body)

    def stage_c(f):
        def weigh(r):
            rows = yrows(r)
            fy[rows, :] = (vy[rows, :].astype(F32) * gy[f, rows, :].astype(F32)).astype(BF16)

        loop(0, ny, weigh)

        def body(r):
            rows = yrows(r)
            dvs[f, rows, :] = jnp.dot(
                dyt[rows, :], fy[...], preferred_element_type=F32
            ).astype(BF16)

        loop(0, ny, body)
        divs(f).start()

    def stage_d(f, s):
        def weigh(m):
            cols = pl.ds(pair_cols(m), pw)
            fz[:, cols] = (visc[:, cols].astype(F32) * gz[f, :, cols].astype(F32)).astype(BF16)

        loop(0, pairs, weigh)
        divs(f).wait()

        def body(m):
            cols = pl.ds(pair_cols(m), pw)
            div = jnp.dot(fz[...], dz[:, cols], preferred_element_type=F32)
            div = div.astype(BF16).astype(F32)
            new = zst[s, :, cols].astype(F32) + 0.5 * (dvr[f, :, cols].astype(F32) + div)
            osend[f, 2 * m, :yl, :] = new[:, :LANES].astype(BF16)
            osend[f, 2 * m + 1, :yl, :] = new[:, 2 * LANES :].astype(BF16)
            top = new[:half, LANES : 2 * LANES]
            bottom = turn(new[half:, LANES : 2 * LANES])
            osend[f, 2 * m, yl:, :] = jnp.where(low, top, bottom).astype(BF16)
            osend[f, 2 * m + 1, yl:, :] = jnp.where(low, bottom, top).astype(BF16)

        loop(0, pairs, body)
        loop(1, nz, lambda d: out_copy(f, lax.rem(me_z + d, nz), me_z).start())
        own_out(f).start()

    for s in range(slots):
        start_in(s)
    w2.wait()
    transpose_dy()
    w1.wait()
    stage_a(0, 0)
    stage_b(0, 0)
    dens_y.start()
    gather_lines(1)
    dens_y.wait()
    viscosity_lines()
    visc_y.start()
    stage_a(1, 2)
    stage_b(1, 2)
    visc_y.wait()

    def field(f):
        stage_c(f)

        @pl.when(f + 2 < fields)
        def _():
            stage_a(f + 2, f + 3)

        stage_d(f, jnp.where(f == 0, 0, f + 1))

        @pl.when(f + 2 < fields)
        def _():
            stage_b(f + 2, f + 3)

    loop(0, fields, field)

    def sent_in(s):
        loop(1, nz, lambda d: in_copy(s, lax.rem(me_z + d, nz), me_z).wait_send())

    loop(0, slots, sent_in)
    dens_y.sent()
    visc_y.sent()

    def finish(f):
        forward(f, jnp.where(f == 0, 0, f + 1)).sent()
        divs(f).sent()

        def body(d):
            other = lax.rem(me_z + nz - d, nz)
            out_copy(f, other, other).wait_recv()
            unfold(f, other)

        own_out(f).wait()
        unfold(f, me_z)
        loop(1, nz, body)
        loop(1, nz, lambda d: out_copy(f, lax.rem(me_z + d, nz), me_z).wait_send())

    loop(0, fields, finish)


def by_planes(nz, ny, state, visc_base, dz_op, dy_op):
    fields, planes, yl, zl = state.shape
    zfull, yfull = dz_op.shape[0], dy_op.shape[0]
    zw = zfull // ny
    slots = fields + 1
    prow = yl + yl // 2
    keep = functools.partial(pltpu.with_memory_space_constraint, memory_space=pltpu.HBM)
    hbm = pl.BlockSpec(memory_space=pltpu.HBM)
    vm = lambda *shape: pltpu.VMEM(shape, BF16)
    dma = lambda *shape: pltpu.SemaphoreType.DMA(shape)
    return pl.pallas_call(
        functools.partial(kernel, nz, ny, fields),
        out_shape=jax.ShapeDtypeStruct(state.shape, BF16),
        in_specs=[hbm] * 4,
        out_specs=pl.BlockSpec(memory_space=pltpu.VMEM),
        scratch_shapes=[
            vm(slots, planes, yl, zl),
            vm(slots, nz, prow, LANES),
            vm(fields, nz, prow, LANES),
            vm(yfull, yfull),
            vm(slots, nz, prow, LANES),
            vm(slots, yl, zfull),
            vm(fields, yfull, zw),
            vm(fields, yl, zfull),
            vm(fields, yfull, zw),
            vm(zfull, zfull),
            vm(yfull, yfull),
            vm(yl, zfull),
            vm(yl, zfull),
            vm(yfull, zw),
            vm(yl, zfull),
            vm(yfull, zw),
            vm(fields, yfull, zw),
            vm(fields, yl, zfull),
            vm(fields, nz, prow, LANES),
            dma(slots, nz), dma(slots, nz),
            dma(fields, ny), dma(fields, ny),
            dma(fields, ny), dma(fields, ny),
            dma(ny), dma(ny), dma(ny), dma(ny),
            dma(fields, nz), dma(fields, nz),
            dma(2), dma(slots),
        ],
        compiler_params=pltpu.CompilerParams(
            collective_id=0, has_side_effects=True, vmem_limit_bytes=46 * 2**20
        ),
    )(keep(state), keep(visc_base), keep(dz_op), keep(dy_op))


def on_device(nz, ny, state, visc_base, dz_op, dy_op):
    planes, yl, zl = visc_base.shape
    if planes == nz and nz % 2 == 0 and zl == LANES + LANES // 2 and yl % 32 == 0:
        if dz_op.shape[0] % (LANES * ny) == 0:
            return by_planes(nz, ny, state, visc_base, dz_op, dy_op)
    return by_lines(state, visc_base, dz_op, dy_op)


def solution(mesh):
    return jax.shard_map(
        functools.partial(on_device, mesh.shape["gz"], mesh.shape["gy"]),
        mesh=mesh,
        in_specs=(P(None, None, "gy", "gz"), P(None, "gy", "gz"), P(), P()),
        out_specs=P(None, None, "gy", "gz"),
        check_vma=False,
    )
```
